128 devices in a mesh: tm: 32 (over y_lo, z, x), feat: 4 (over y_hi, core).
Axes of the slice: x: 4, y: 4 (y_hi: 2, y_lo: 2; y = y_hi * 2 + y_lo), z: 4, core: 2. Of those that a mesh axis runs over, the one named last changes fastest.
Arguments:
- coords: float32 [2048, 3, 8, 256], P('tm'), may hold values from -12 to 12, as said below
- set_a: int32 [128], replicated, may hold values from 0 to 255
- set_b: int32 [128], replicated, may hold values from 0 to 255
Outputs:
- c00: float32 [16384, 16384], P('feat', 'tm')
- c0t: float32 [16384, 16384], P('feat', 'tm')
The draws below stay inside these ranges and needn't reach their ends.
Inputs may be any that keep to these rules, and one draw needn't show every extreme that they name: `coords`: positions of a folding protein.
All inputs are finite; a program needn't handle non-finite values.
Results may differ from the reference program's by a relative error of at most 0.0003.
Values may be sent and summed in bfloat16 or wider, within the bound.
No kernel may reach another device: no remote copies, remote signals or barrier semaphores. Data moves between devices by JAX's collectives and lax.ppermute only.
A program may use at most 128 MiB of HBM per device.

```python
import jax
import jax.numpy as jnp
from jax import lax

RES = 256
ATOMS = 8
NA = 128
NB = 128
LAG = 64
FR_DEV = 64
FRAMES = 2048


def draw_coords(key, part):
    keys = jax.random.split(key, 5)
    centers = jax.random.normal(keys[0], (3, 1, RES), jnp.float32) * 0.9
    offsets = jax.random.normal(keys[1], (3, ATOMS, RES), jnp.float32) * 0.2
    relax = jnp.exp(jax.random.uniform(keys[2], (1, ATOMS, RES), jnp.float32, 0.0, jnp.log(512.0)))
    factor = jnp.exp(-1.0 / relax)
    noise = jax.random.normal(keys[3], (FRAMES, 3, ATOMS, RES), jnp.float32)
    jitter = jax.random.normal(keys[4], (FRAMES, 3, ATOMS, RES), jnp.float32) * 0.3
    spread = 0.3
    ramp = 1.5 - 0.8 * jnp.arange(FRAMES, dtype=jnp.float32) / max(FRAMES - 1, 1)
    kick = jnp.sqrt(1.0 - factor * factor) * spread

    def advance(state, fresh):
        updated = factor * state + kick * fresh
        return (updated, updated)
    start = noise[0] * spread
    final_state, moves = lax.scan(advance, start, noise)
    positions = ramp[:, None, None, None] * centers[None] + offsets[None] + moves + jitter
    return jnp.clip(positions, -12.0, 12.0).astype(jnp.float32)


def touch_ends(array, key, least, top_value):
    extent = array.shape
    place = [jax.random.randint(jax.random.fold_in(key, axis), (), 0, extent[axis]) for axis in range(len(extent))]
    array = array.at[tuple(place)].set(least)
    longest = extent.index(max(extent))
    place[longest] = (place[longest] + 1) % extent[longest]
    return array.at[tuple(place)].set(top_value)


def setup_inputs(seed: int = 0) -> dict:
    key_of = jax.random.split(jax.random.key(seed), 4)
    coords = draw_coords(jax.random.fold_in(key_of[3], 71), 0)
    set_a = touch_ends(jax.random.randint(key_of[1], (NA,), 0, RES), jax.random.fold_in(key_of[1], 1), 0, RES - 1).astype(jnp.int32)
    set_b = touch_ends(jax.random.randint(key_of[2], (NB,), 0, RES), jax.random.fold_in(key_of[2], 1), 0, RES - 1).astype(jnp.int32)
    return dict(coords=coords, set_a=set_a, set_b=set_b)


contact_radius = 1.2
contact_width = 0.25

def contact_features(positions, index_a, index_b):
    part_a = jnp.take(positions, index_a, axis=3)
    part_b = jnp.take(positions, index_b, axis=3)
    frame_rows = positions.shape[0]
    summed = jnp.zeros((frame_rows, part_a.shape[3], part_b.shape[3]), jnp.float32)
    for first_atom in range(part_a.shape[2]):
        square = jnp.zeros((frame_rows, part_b.shape[2], part_a.shape[3], part_b.shape[3]), jnp.float32)
        for component in range(3):
            difference = part_a[:, component, first_atom, :][:, None, :, None] - part_b[:, component, :, :][:, :, None, :]
            square = square + difference * difference
        summed = summed + lax.optimization_barrier(jnp.sum(jax.nn.sigmoid((contact_radius - jnp.sqrt(square)) / contact_width), axis=1))
    summed = summed / float(part_a.shape[2])
    return summed.reshape(frame_rows, part_a.shape[3] * part_b.shape[3])

def contract_frames(left, right):
    return lax.dot_general(left.astype(jnp.float32), right.astype(jnp.float32), (((0,), (0,)), ((), ())), precision=lax.Precision.HIGHEST, preferred_element_type=jnp.float32)

def reference(coords, set_a, set_b):
    blocks = coords.reshape(FRAMES // FR_DEV, FR_DEV, 3, ATOMS, RES)
    lifted = lax.map(lambda block: contact_features(block, set_a, set_b), blocks).reshape(FRAMES, NA * NB)
    pairs = FRAMES - LAG
    frame_ids = jnp.arange(FRAMES, dtype=jnp.int32)
    weight = (frame_ids < pairs).astype(jnp.float32) + (frame_ids >= LAG).astype(jnp.float32)
    means = jnp.dot(weight, lifted, precision=lax.Precision.HIGHEST) / (2.0 * pairs)
    centered = (lifted - means[None, :]).astype(jnp.bfloat16)
    centered = lax.optimization_barrier(centered)
    early = centered[:pairs].astype(jnp.float32)
    later = centered[LAG:].astype(jnp.float32)
    plus = (early + later).astype(jnp.bfloat16)
    minus = (early - later).astype(jnp.bfloat16)
    sum_plus = contract_frames(plus, plus)
    sum_minus = contract_frames(minus, minus)
    c00 = (sum_plus + sum_minus) / (4.0 * pairs)
    c0t = (sum_plus - sum_minus) / (4.0 * pairs)
    return (c00, c0t)
```

```python
import jax
import jax.numpy as jnp
from jax import lax
from jax.experimental import pallas as pl
from jax.experimental.pallas import tpu as pltpu
from jax.sharding import Mesh, PartitionSpec as P

LAG = 64
contact_radius = 1.2
contact_width = 0.25
CHUNKS = 2
TILE = 256
MIB = 1 << 20


def feature_kernel(count, first, index_ref, coords_ref, lifted_ref, sums_ref, part_a, part_b):
    frames = coords_ref.shape[1]
    atoms = coords_ref.shape[0] // 3
    index_a = jnp.broadcast_to(index_ref[0:1, :], (8, 128))
    index_b = jnp.broadcast_to(index_ref[1:2, :], (8, 128))

    def lanes(array, index):
        return jnp.take_along_axis(array, index, axis=1, mode="promise_in_bounds")

    def chosen(low, high, index):
        return jnp.where(index < 128, lanes(low, index & 127), lanes(high, index & 127))

    scale = 0.5 / contact_width
    shift = contact_radius * scale

    @pl.loop(0, frames // 8)
    def _(octet):
        rows = pl.ds(pl.multiple_of(octet * 8, 8), 8)
        for piece in range(3 * atoms):
            both = coords_ref[piece, rows, :] * scale
            low, high = both[:, :128], both[:, 128:]
            part_a[piece] = chosen(low, high, index_a)
            part_b[piece] = chosen(low, high, index_b)

        @pl.loop(0, count)
        def _(residue):
            at = jnp.full((8, 128), first + residue, jnp.int32)
            total = None
            for p in range(atoms):
                ax, ay, az = [lanes(part_a[c * atoms + p], at) for c in range(3)]
                for q in range(atoms):
                    dx = ax - part_b[q]
                    dy = ay - part_b[atoms + q]
                    dz = az - part_b[2 * atoms + q]
                    square = jnp.maximum(dx * dx + dy * dy + dz * dz, 1e-30)
                    value = jnp.tanh(shift - square * lax.rsqrt(square))
                    total = value if total is None else total + value
            features = (total + float(atoms * atoms)) * (0.5 / atoms)
            lifted_ref[rows, pl.ds(pl.multiple_of(residue * 128, 128), 128)] = features

    sums_ref[...] = jnp.sum(lifted_ref[...], axis=0, keepdims=True) * index_ref[2:3, 0:1].astype(jnp.float32)


def contact_features(count, first, indices, coords):
    pieces, frames, residues = coords.shape
    width = count * 128
    pairs = frames * width * (pieces // 3) ** 2
    return pl.pallas_call(
        lambda *refs: feature_kernel(count, first, *refs),
        out_shape=(
            jax.ShapeDtypeStruct((frames, width), jnp.float32),
            jax.ShapeDtypeStruct((1, width), jnp.float32),
        ),
        in_specs=[pl.BlockSpec(memory_space=pltpu.VMEM)] * 2,
        out_specs=[pl.BlockSpec(memory_space=pltpu.VMEM)] * 2,
        scratch_shapes=[pltpu.VMEM((pieces, 8, 128), jnp.float32)] * 2,
        compiler_params=pltpu.CompilerParams(vmem_limit_bytes=24 * MIB),
        cost_estimate=pl.CostEstimate(flops=pairs * 12, bytes_accessed=4 * MIB, transcendentals=2 * pairs),
    )(indices, coords)


def column_kernel(map_ref, cols_ref, out_ref):
    blocks, frames, width = cols_ref.shape

    @pl.loop(0, blocks)
    def _(block):
        here = cols_ref[map_ref[block]].astype(jnp.float32)
        before = cols_ref[map_ref[jnp.maximum(block - 1, 0)]].astype(jnp.float32)
        after = cols_ref[map_ref[jnp.minimum(block + 1, blocks - 1)]].astype(jnp.float32)
        inner = jnp.logical_and(block > 0, block < blocks - 1)
        out_ref[block, :, :width] = jnp.where(inner, 2.0 * here, here).astype(jnp.bfloat16)
        lagged = jnp.where(block > 0, before, 0.0) + jnp.where(block < blocks - 1, after, 0.0)
        out_ref[block, :, width:] = lagged.astype(jnp.bfloat16)


def lagged_columns(block_map, cols):
    blocks, frames, width = cols.shape
    return pl.pallas_call(
        column_kernel,
        out_shape=jax.ShapeDtypeStruct((blocks, frames, 2 * width), jnp.bfloat16),
        in_specs=[pl.BlockSpec(memory_space=pltpu.SMEM), pl.BlockSpec(memory_space=pltpu.VMEM)],
        out_specs=pl.BlockSpec(memory_space=pltpu.VMEM),
        compiler_params=pltpu.CompilerParams(vmem_limit_bytes=24 * MIB),
        cost_estimate=pl.CostEstimate(flops=8 * cols.size, bytes_accessed=6 * cols.size, transcendentals=0),
    )(block_map, cols)


def product_kernel(sizes, factor, aliased, map_ref, *refs):
    pieces = refs[: len(sizes)]
    columns_ref = refs[len(sizes)]
    c00_ref, c0t_ref, gathered = refs[len(sizes) + 1 + aliased :]
    frames = columns_ref.shape[1]
    width = c00_ref.shape[1]
    place = 0
    for size, piece in zip(sizes, pieces):
        for shard in range(size):
            start = pl.multiple_of(map_ref[place] * frames, frames)
            gathered[pl.ds(start, frames), :] = piece[shard]
            place += 1
    columns = columns_ref[...].reshape(gathered.shape[0], 2 * width)
    sums = lax.dot_general(
        gathered[...], columns, (((0,), (0,)), ((), ())), preferred_element_type=jnp.float32
    )
    c00_ref[...] = sums[:, :width] * factor
    c0t_ref[...] = sums[:, width:] * factor


def products(block_map, pieces, columns, row_start, rows, factor, previous):
    blocks, frames, double = columns.shape
    width = double // 2
    features = pieces[0].shape[2]
    sizes = [piece.shape[0] for piece in pieces]
    first = row_start // TILE
    out = jax.ShapeDtypeStruct((rows, width), jnp.float32)
    count = len(sizes)
    passed = () if previous is None else previous
    in_specs = [pl.BlockSpec(memory_space=pltpu.SMEM)]
    in_specs += [pl.BlockSpec((size, frames, TILE), lambda i: (0, 0, i)) for size in sizes]
    in_specs += [pl.BlockSpec((blocks, frames, double), lambda i: (0, 0, 0))]
    in_specs += [pl.BlockSpec(memory_space=pl.ANY)] * len(passed)
    return pl.pallas_call(
        lambda *refs: product_kernel(sizes, factor, len(passed), *refs),
        grid=(features // TILE,),
        out_shape=(out, out),
        in_specs=in_specs,
        out_specs=[pl.BlockSpec((TILE, width), lambda i: (first + i, 0))] * 2,
        scratch_shapes=[pltpu.VMEM((blocks * frames, TILE), jnp.bfloat16)],
        input_output_aliases={count + 2 + n: n for n in range(len(passed))},
        compiler_params=pltpu.CompilerParams(vmem_limit_bytes=40 * MIB),
        cost_estimate=pl.CostEstimate(
            flops=2 * features * blocks * frames * double,
            bytes_accessed=features * blocks * frames * 2 + features * double * 4 + columns.size * 2,
            transcendentals=0,
        ),
    )(block_map, *pieces, columns, *passed)


def moved(array, axis, by):
    length = lax.axis_size(axis)
    return lax.ppermute(array, axis, [(i, (i + by) % length) for i in range(length)])


def summed(array):
    for axis, flip in (("x", 1), ("x", 2), ("z", 1), ("z", 2), ("yl", 1)):
        length = lax.axis_size(axis)
        array = array + lax.ppermute(array, axis, [(i, i ^ flip) for i in range(length)])
    return array


def around(block, axis):
    half = block.shape[0] // 2
    behind = moved(block, axis, 1)
    ahead = moved(block, axis, -1)
    far_first = moved(behind[:half], axis, 1)
    far_last = moved(ahead[half:], axis, -1)
    return (block, behind, ahead, far_first, far_last)


def gathered_rows(block, first, second):
    plane = jnp.concatenate(around(block, first), axis=0)
    return around(plane, second)


def row_order(first, second, outer_is_z, place):
    partner = [place["yl"], 1 - place["yl"]]
    line = []
    for offset in (0, -1, 1):
        line += [((place[first] + offset) % 4, y) for y in partner]
    line += [((place[first] + 2) % 4, y) for y in partner]
    whole = []
    half = len(line) // 2
    for offset in (0, -1, 1):
        whole += [((place[second] + offset) % 4, one, y) for one, y in line]
    whole += [((place[second] + 2) % 4, one, y) for one, y in line]
    order = []
    for two, one, y in whole:
        z, x = (two, one) if outer_is_z else (one, two)
        order.append(y * 16 + z * 4 + x)
    return jnp.stack(order).astype(jnp.int32)


def own_columns(centered, place):
    frames, features = centered.shape
    width = features // 8
    by_owner = jnp.transpose(centered.reshape(frames, 2, 4, width), (2, 1, 0, 3))
    along_x = [lax.dynamic_index_in_dim(by_owner, place["x"], 0, keepdims=False)]
    for by in (1, 2, 3):
        piece = lax.dynamic_index_in_dim(by_owner, (place["x"] + by) % 4, 0, keepdims=False)
        along_x.append(moved(piece, "x", by))
    along_x = jnp.stack(along_x)
    along_z = [lax.dynamic_index_in_dim(along_x, place["z"] % 2, 1, keepdims=False)]
    for by in (1, 2, 3):
        piece = lax.dynamic_index_in_dim(along_x, (place["z"] + by) % 2, 1, keepdims=False)
        pairs = []
        for z in range(4):
            target = (z + by) % 4
            core = target // 2
            pairs.append((z * 2 + core, target * 2 + core))
        along_z.append(lax.ppermute(piece, ("z", "c"), pairs))
    along_z = jnp.stack(along_z)

    def along_y(moves):
        pairs = []
        for z in range(4):
            for source, target in moves:
                flat = lambda y: (((y % 2) * 4 + z) * 2 + y // 2) * 2 + z // 2
                pairs.append((flat(source), flat(target)))
        return lax.ppermute(along_z, ("yl", "z", "yh", "c"), pairs)

    one = along_y([(0, 2), (1, 0), (2, 3), (3, 1)])
    two = along_y([(1, 2), (2, 1)])
    two = jnp.where(place["yl"] == place["yh"], along_z, two)
    both = jnp.stack([one, two])
    pairs = [(z * 2 + z // 2, z * 2 + 1 - z // 2) for z in range(4)]
    passed = lax.ppermute(both, ("z", "c"), pairs)
    both = jnp.where(place["z"] // 2 == place["c"], both, passed)
    order = []
    for block in range(32):
        y, z, x = block // 16, (block // 4) % 4, block % 4
        group = jnp.where(y == 1 - place["yh"], 0, 1)
        order.append(group * 16 + ((place["z"] - z) % 4) * 4 + (place["x"] - x) % 4)
    return both.reshape(32, frames, width), jnp.stack(order).astype(jnp.int32)


def per_device(coords, set_a, set_b):
    place = {axis: lax.axis_index(axis) for axis in ("yl", "z", "x", "yh", "c")}
    frames, _, atoms, residues = coords.shape
    feat_index = place["yh"] * 2 + place["c"]
    time_index = place["yl"] * 16 + place["z"] * 4 + place["x"]
    rows_a = set_a.shape[0] // 4
    pairs = frames * 32 - LAG
    edge = jnp.logical_or(time_index == 0, time_index == 31)
    index_a = lax.dynamic_slice_in_dim(set_a, feat_index * rows_a, rows_a)
    index_a = jnp.concatenate([index_a, jnp.zeros((128 - rows_a,), jnp.int32)])
    weight = jnp.broadcast_to(jnp.where(edge, 1, 2).astype(jnp.int32), (128,))
    indices = jnp.stack([index_a, set_b, weight, *([weight] * 5)])
    atoms_first = jnp.transpose(coords, (1, 2, 0, 3)).reshape(3 * atoms, frames, residues)

    count = rows_a // CHUNKS
    features = count * 128
    chunks = []
    for chunk in range(CHUNKS):
        lifted, sums = contact_features(count, chunk * count, indices, atoms_first)
        means = summed(sums) / (2.0 * pairs)
        chunks.append((lifted - means).astype(jnp.bfloat16))

    cols, col_order = own_columns(jnp.concatenate(chunks, axis=1), place)
    columns = lagged_columns(col_order, cols)

    rows = rows_a * 128
    results = None
    half = features // 2
    for chunk in range(CHUNKS):
        partner = moved(chunks[chunk], "yl", 1)
        block = jnp.stack([chunks[chunk], partner])
        for part, (first, second) in enumerate((("x", "z"), ("z", "x"))):
            pieces = gathered_rows(block[:, :, part * half : (part + 1) * half], first, second)
            order = row_order(first, second, second == "z", place)
            start = chunk * features + part * half
            results = products(order, pieces, columns, start, rows, 1.0 / (2.0 * pairs), results)
    return results


def solution(mesh):
    fine = Mesh(mesh.devices.reshape(2, 4, 4, 2, 2), ("yl", "z", "x", "yh", "c"))
    time_axes, feat_axes = ("yl", "z", "x"), ("yh", "c")
    return jax.shard_map(
        per_device,
        mesh=fine,
        in_specs=(P(time_axes, None, None, None), P(), P()),
        out_specs=(P(feat_axes, time_axes), P(feat_axes, time_axes)),
        check_vma=False,
    )
```

```python
import jax
import jax.numpy as jnp
from jax import lax
from jax.experimental import pallas as pl
from jax.experimental.pallas import tpu as pltpu
from jax.sharding import Mesh, PartitionSpec as P

LAG = 64
contact_radius = 1.2
contact_width = 0.25
TILE = 512
MIB = 1 << 20


def feature_kernel(index_ref, coords_ref, lifted_ref, sums_ref, chosen):
    rows_all, residues = coords_ref.shape
    frames, width = lifted_ref.shape
    pieces = rows_all // frames
    atoms = pieces // 3
    scale = 0.5 / contact_width
    shift = contact_radius * scale

    numbers = lax.broadcasted_iota(jnp.int32, (residues, 256), 0)
    one_hot = jnp.where(numbers == index_ref[0:1, :], scale, 0.0).astype(jnp.bfloat16)

    @pl.loop(0, 3)
    def _(component):
        rows = pl.ds(pl.multiple_of(component * (atoms * frames), atoms * frames), atoms * frames)
        whole = coords_ref[rows, :]
        high = whole.astype(jnp.bfloat16)
        rest = whole - high.astype(jnp.float32)
        middle = rest.astype(jnp.bfloat16)
        low = (rest - middle.astype(jnp.float32)).astype(jnp.bfloat16)
        parts = [jnp.dot(part, one_hot, preferred_element_type=jnp.float32) for part in (high, middle, low)]
        chosen[rows, :] = (parts[0] + parts[1]) + parts[2]

    @pl.loop(0, frames // 8)
    def _(octet):
        start = pl.multiple_of(octet * 8, 8)
        for residue in range(width // 128):
            totals = [None, None]
            for p in range(atoms):
                ax, ay, az = [
                    jnp.broadcast_to(
                        chosen[pl.ds((c * atoms + p) * frames + start, 8), 128 + residue : 129 + residue], (8, 128)
                    )
                    for c in range(3)
                ]
                for q in range(atoms):
                    bx, by, bz = [chosen[pl.ds((c * atoms + q) * frames + start, 8), :128] for c in range(3)]
                    dx, dy, dz = ax - bx, ay - by, az - bz
                    square = jnp.maximum(dx * dx + dy * dy + dz * dz, 1e-30)
                    value = jnp.tanh(shift - square * lax.rsqrt(square))
                    totals[q % 2] = value if totals[q % 2] is None else totals[q % 2] + value
            features = (totals[0] + totals[1] + float(atoms * atoms)) * (0.5 / atoms)
            lifted_ref[pl.ds(start, 8), residue * 128 : (residue + 1) * 128] = features

    weight = index_ref[1:2, 0:1].astype(jnp.float32)
    sums_ref[...] = jnp.sum(lifted_ref[...], axis=0, keepdims=True) * weight


def contact_features(count, indices, coords):
    pieces, frames, residues = coords.shape
    width = count * 128
    pairs = frames * width * (pieces // 3) ** 2
    return pl.pallas_call(
        feature_kernel,
        out_shape=(
            jax.ShapeDtypeStruct((frames, width), jnp.float32),
            jax.ShapeDtypeStruct((1, width), jnp.float32),
        ),
        in_specs=[pl.BlockSpec(memory_space=pltpu.VMEM)] * 2,
        out_specs=[pl.BlockSpec(memory_space=pltpu.VMEM)] * 2,
        scratch_shapes=[pltpu.VMEM((pieces * frames, 256), jnp.float32)],
        compiler_params=pltpu.CompilerParams(vmem_limit_bytes=24 * MIB),
        cost_estimate=pl.CostEstimate(flops=pairs * 12, bytes_accessed=4 * MIB, transcendentals=2 * pairs),
    )(indices, coords.reshape(pieces * frames, residues))


def column_kernel(map_ref, orders_ref, cols_ref, *out_refs):
    blocks, frames, width = cols_ref.shape

    @pl.loop(0, blocks)
    def _(number):
        for stream, out_ref in enumerate(out_refs):
            block = orders_ref[stream, number]
            here = cols_ref[map_ref[block]].astype(jnp.float32)
            before = cols_ref[map_ref[jnp.maximum(block - 1, 0)]].astype(jnp.float32)
            after = cols_ref[map_ref[jnp.minimum(block + 1, blocks - 1)]].astype(jnp.float32)
            inner = jnp.logical_and(block > 0, block < blocks - 1)
            out_ref[number, :, :width] = jnp.where(inner, 2.0 * here, here).astype(jnp.bfloat16)
            lagged = jnp.where(block > 0, before, 0.0) + jnp.where(block < blocks - 1, after, 0.0)
            out_ref[number, :, width:] = lagged.astype(jnp.bfloat16)


def lagged_columns(block_map, orders, cols):
    blocks, frames, width = cols.shape
    out = jax.ShapeDtypeStruct((blocks, frames, 2 * width), jnp.bfloat16)
    return pl.pallas_call(
        column_kernel,
        out_shape=(out, out),
        in_specs=[pl.BlockSpec(memory_space=pltpu.SMEM)] * 2 + [pl.BlockSpec(memory_space=pltpu.VMEM)],
        out_specs=[pl.BlockSpec(memory_space=pltpu.VMEM)] * 2,
        compiler_params=pltpu.CompilerParams(vmem_limit_bytes=24 * MIB),
        cost_estimate=pl.CostEstimate(flops=16 * cols.size, bytes_accessed=10 * cols.size, transcendentals=0),
    )(block_map, orders, cols)


def product_kernel(count, factor, added, *refs):
    pieces, columns_ref = refs[:count], refs[count]
    c00_ref, c0t_ref = refs[-2:]
    width = c00_ref.shape[1]
    left = jnp.concatenate([piece[...].reshape(-1, piece.shape[2]) for piece in pieces], axis=0)
    right = columns_ref[...].reshape(left.shape[0], 2 * width)
    sums = lax.dot_general(left, right, (((0,), (0,)), ((), ())), preferred_element_type=jnp.float32)
    for number, ref in enumerate((c00_ref, c0t_ref)):
        part = sums[:, number * width : (number + 1) * width] * factor
        ref[...] = part + refs[count + 1 + number][...] if added else part


def products(pieces, columns, column_start, row_start, rows, factor, previous, added):
    _, frames, double = columns.shape
    width = double // 2
    features = pieces[0].shape[2]
    first = row_start // TILE
    out = jax.ShapeDtypeStruct((rows, width), jnp.float32)
    count = len(pieces)
    blocks = sum(piece.shape[0] for piece in pieces)
    passed = () if previous is None else previous
    out_spec = pl.BlockSpec((TILE, width), lambda i: (first + i, 0))
    in_specs = [pl.BlockSpec((piece.shape[0], frames, TILE), lambda i: (0, 0, i)) for piece in pieces]
    in_specs += [pl.BlockSpec((blocks, frames, double), lambda i: (column_start // blocks, 0, 0))]
    in_specs += [out_spec if added else pl.BlockSpec(memory_space=pl.ANY)] * len(passed)
    return pl.pallas_call(
        lambda *refs: product_kernel(count, factor, added, *refs),
        grid=(features // TILE,),
        in_specs=in_specs,
        out_specs=[out_spec] * 2,
        out_shape=(out, out),
        input_output_aliases={count + 1 + n: n for n in range(len(passed))},
        compiler_params=pltpu.CompilerParams(vmem_limit_bytes=36 * MIB),
        cost_estimate=pl.CostEstimate(
            flops=2 * features * blocks * frames * double,
            bytes_accessed=features * double * (8 if added else 4) + blocks * frames * (features + double) * 2,
            transcendentals=0,
        ),
    )(*pieces, columns, *passed)


def plane_kernel(*refs):
    for number, ref in enumerate(refs[:-1]):
        refs[-1][number] = ref[...]


def plane_of(blocks):
    return pl.pallas_call(
        plane_kernel,
        out_shape=jax.ShapeDtypeStruct((len(blocks), *blocks[0].shape), blocks[0].dtype),
        in_specs=[pl.BlockSpec(memory_space=pltpu.VMEM)] * len(blocks),
        out_specs=pl.BlockSpec(memory_space=pltpu.VMEM),
        compiler_params=pltpu.CompilerParams(vmem_limit_bytes=16 * MIB),
        cost_estimate=pl.CostEstimate(
            flops=0, bytes_accessed=4 * len(blocks) * blocks[0].size, transcendentals=0
        ),
    )(*blocks)


def moved(array, axis, by):
    length = lax.axis_size(axis)
    return lax.ppermute(array, axis, [(i, (i + by) % length) for i in range(length)])


def summed(array):
    for axis in ("x", "z", "yl"):
        steps = range(1, lax.axis_size(axis))
        array = sum([moved(array, axis, by) for by in steps], start=array)
    return array


OFFSETS = (0, -1, 1, 2)


def near_blocks(block, axis):
    return moved(block, axis, 1), moved(block, axis, -1)


def far_block(behind, ahead, axis):
    half = behind.shape[0] // 2
    return moved(behind[:half], axis, 1), moved(ahead[half:], axis, -1)


def block_order(first, second, place):
    order = []
    for offset in OFFSETS:
        for yl in (place["yl"], 1 - place["yl"]):
            for inner in OFFSETS:
                at = {first: (place[first] + inner) % 4, second: (place[second] + offset) % 4}
                order.append(yl * 16 + at["z"] * 4 + at["x"])
    return jnp.stack(order).astype(jnp.int32)


def columns_along_x(centered, place):
    frames, features = centered.shape
    by_owner = jnp.transpose(centered.reshape(frames, 2, 4, features // 8), (2, 1, 0, 3))
    along_x = [lax.dynamic_index_in_dim(by_owner, place["x"], 0, keepdims=False)]
    for by in (1, 2, 3):
        piece = lax.dynamic_index_in_dim(by_owner, (place["x"] + by) % 4, 0, keepdims=False)
        along_x.append(moved(piece, "x", by))
    return along_x


def columns_along_z(along_x, place):
    along_x = jnp.stack(along_x)
    along_z = [lax.dynamic_index_in_dim(along_x, place["z"] % 2, 1, keepdims=False)]
    for by in (1, 2, 3):
        piece = lax.dynamic_index_in_dim(along_x, (place["z"] + by) % 2, 1, keepdims=False)
        pairs = []
        for z in range(4):
            target = (z + by) % 4
            core = target // 2
            pairs.append((z * 2 + core, target * 2 + core))
        along_z.append(lax.ppermute(piece, ("z", "c"), pairs))
    return along_z


def columns_along_y(along_z, moves):
    pairs = []
    for z in range(4):
        for source, target in moves:
            flat = lambda y: (((y % 2) * 4 + z) * 2 + y // 2) * 2 + z // 2
            pairs.append((flat(source), flat(target)))
    return lax.ppermute(along_z, ("yl", "z", "yh", "c"), pairs)


def columns_of_chip(one, two, place):
    both = jnp.stack([one, two])
    pairs = [(z * 2 + z // 2, z * 2 + 1 - z // 2) for z in range(4)]
    passed = lax.ppermute(both, ("z", "c"), pairs)
    both = jnp.where(place["z"] // 2 == place["c"], both, passed)
    order = []
    for block in range(32):
        y, z, x = block // 16, (block // 4) % 4, block % 4
        group = jnp.where(y == 1 - place["yh"], 0, 1)
        order.append(group * 16 + ((place["z"] - z) % 4) * 4 + (place["x"] - x) % 4)
    return both.reshape(32, *both.shape[3:]), jnp.stack(order).astype(jnp.int32)


def together(*groups):
    return lax.optimization_barrier(groups)


def per_device(coords, set_a, set_b):
    place = {axis: lax.axis_index(axis) for axis in ("yl", "z", "x", "yh", "c")}
    frames, _, atoms, residues = coords.shape
    feat_index = place["yh"] * 2 + place["c"]
    time_index = place["yl"] * 16 + place["z"] * 4 + place["x"]
    rows_a = set_a.shape[0] // 4
    pairs = frames * 32 - LAG
    edge = jnp.logical_or(time_index == 0, time_index == 31)
    index_a = lax.dynamic_slice_in_dim(set_a, feat_index * rows_a, rows_a)
    chosen = jnp.concatenate([set_b, index_a, jnp.zeros((128 - rows_a,), jnp.int32)])
    weight = jnp.broadcast_to(jnp.where(edge, 1, 2).astype(jnp.int32), (256,))
    indices = jnp.stack([chosen, weight, *([weight] * 6)])
    atoms_first = jnp.transpose(coords, (1, 2, 0, 3)).reshape(3 * atoms, frames, residues)

    lifted, sums = contact_features(rows_a, indices, atoms_first)
    centered = (lifted - summed(sums) / (2.0 * pairs)).astype(jnp.bfloat16)

    rows = rows_a * 128
    half = rows // 2
    ways = (("x", "z"), ("z", "x"))
    taken = (slice(0, half), slice(half, rows))

    own = [centered[:, part] for part in taken]
    partner = moved(centered, "yl", 1)
    own_near = [near_blocks(block, way[0]) for block, way in zip(own, ways)]
    along_x = columns_along_x(centered, place)
    partner, own_near, own, along_x = together(partner, own_near, own, along_x)

    other = [partner[:, part] for part in taken]
    other_near = [near_blocks(block, way[0]) for block, way in zip(other, ways)]
    along_z = jnp.stack(columns_along_z(along_x, place))
    other_near, along_z, own_near, other = together(other_near, along_z, own_near, other)

    far = [
        (moved(mine[0], way[0], 1), moved(theirs[1], way[0], -1))
        for mine, theirs, way in zip(own_near, other_near, ways)
    ]
    one = columns_along_y(along_z, [(0, 2), (1, 0), (2, 3), (3, 1)])
    far, along_z, one = together(far, along_z, one)

    planes = [
        plane_of([own[n], *own_near[n], far[n][0], other[n], *other_near[n], far[n][1]]) for n in range(2)
    ]
    planes, along_z = together(planes, along_z)
    near = [near_blocks(plane, way[1]) for plane, way in zip(planes, ways)]
    two = columns_along_y(along_z, [(1, 2), (2, 1)])
    two = jnp.where(place["yl"] == place["yh"], along_z, two)
    cols, col_order = columns_of_chip(one, two, place)
    orders = jnp.stack([block_order(*way, place) for way in ways])
    columns = lagged_columns(col_order, orders, cols)

    last = [far_block(*blocks, way[1]) for blocks, way in zip(near, ways)]
    results = None
    for n in range(2):
        results = products([planes[n], *near[n]], columns[n], 0, n * half, rows, 0.5 / pairs, results, False)
    for n in range(2):
        results = products(last[n], columns[n], 24, n * half, rows, 0.5 / pairs, results, True)
    return results


def solution(mesh):
    fine = Mesh(mesh.devices.reshape(2, 4, 4, 2, 2), ("yl", "z", "x", "yh", "c"))
    time_axes, feat_axes = ("yl", "z", "x"), ("yh", "c")
    return jax.shard_map(
        per_device,
        mesh=fine,
        in_specs=(P(time_axes, None, None, None), P(), P()),
        out_specs=(P(feat_axes, time_axes), P(feat_axes, time_axes)),
        check_vma=False,
    )
```

```python
import jax
import jax.numpy as jnp
from jax import lax
from jax.experimental import pallas as pl
from jax.experimental.pallas import tpu as pltpu
from jax.sharding import Mesh, PartitionSpec as P

LAG = 64
contact_radius = 1.2
contact_width = 0.25
TILE = 512
MIB = 1 << 20


def feature_kernel(index_ref, coords_ref, lifted_ref, sums_ref, chosen):
    rows_all, residues = coords_ref.shape
    frames, width = lifted_ref.shape
    pieces = rows_all // frames
    atoms = pieces // 3
    scale = 0.5 / contact_width
    shift = contact_radius * scale

    numbers = lax.broadcasted_iota(jnp.int32, (residues, 256), 0)
    one_hot = jnp.where(numbers == index_ref[0:1, :], scale, 0.0).astype(jnp.bfloat16)

    @pl.loop(0, 3)
    def _(component):
        rows = pl.ds(pl.multiple_of(component * (atoms * frames), atoms * frames), atoms * frames)
        whole = coords_ref[rows, :]
        high = whole.astype(jnp.bfloat16)
        rest = whole - high.astype(jnp.float32)
        middle = rest.astype(jnp.bfloat16)
        low = (rest - middle.astype(jnp.float32)).astype(jnp.bfloat16)
        parts = [jnp.dot(part, one_hot, preferred_element_type=jnp.float32) for part in (high, middle, low)]
        chosen[rows, :] = (parts[0] + parts[1]) + parts[2]

    @pl.loop(0, frames // 8)
    def _(octet):
        start = pl.multiple_of(octet * 8, 8)
        for residue in range(width // 128):
            totals = [None, None]
            for p in range(atoms):
                ax, ay, az = [
                    jnp.broadcast_to(
                        chosen[pl.ds((c * atoms + p) * frames + start, 8), 128 + residue : 129 + residue], (8, 128)
                    )
                    for c in range(3)
                ]
                for q in range(atoms):
                    bx, by, bz = [chosen[pl.ds((c * atoms + q) * frames + start, 8), :128] for c in range(3)]
                    dx, dy, dz = ax - bx, ay - by, az - bz
                    square = jnp.maximum(dx * dx + dy * dy + dz * dz, 1e-30)
                    value = jnp.tanh(shift - square * lax.rsqrt(square))
                    totals[q % 2] = value if totals[q % 2] is None else totals[q % 2] + value
            features = (totals[0] + totals[1] + float(atoms * atoms)) * (0.5 / atoms)
            lifted_ref[pl.ds(start, 8), residue * 128 : (residue + 1) * 128] = features

    weight = index_ref[1:2, 0:1].astype(jnp.float32)
    sums_ref[...] = jnp.sum(lifted_ref[...], axis=0, keepdims=True) * weight


def contact_features(count, indices, coords):
    pieces, frames, residues = coords.shape
    width = count * 128
    pairs = frames * width * (pieces // 3) ** 2
    return pl.pallas_call(
        feature_kernel,
        out_shape=(
            jax.ShapeDtypeStruct((frames, width), jnp.float32),
            jax.ShapeDtypeStruct((1, width), jnp.float32),
        ),
        in_specs=[pl.BlockSpec(memory_space=pltpu.VMEM)] * 2,
        out_specs=[pl.BlockSpec(memory_space=pltpu.VMEM)] * 2,
        scratch_shapes=[pltpu.VMEM((pieces * frames, 256), jnp.float32)],
        compiler_params=pltpu.CompilerParams(vmem_limit_bytes=24 * MIB),
        cost_estimate=pl.CostEstimate(flops=pairs * 12, bytes_accessed=4 * MIB, transcendentals=2 * pairs),
    )(indices, coords.reshape(pieces * frames, residues))


def column_kernel(map_ref, places_ref, own_ref, passed_ref, *out_refs):
    blocks, frames, width = own_ref.shape

    def fill(cols_ref, skipped):
        def block_at(number):
            return cols_ref[map_ref[number] - skipped].astype(jnp.float32)

        @pl.loop(0, blocks)
        def _(block):
            here = block_at(block)
            before = block_at(jnp.maximum(block - 1, 0))
            after = block_at(jnp.minimum(block + 1, blocks - 1))
            inner = jnp.logical_and(block > 0, block < blocks - 1)
            weighted = jnp.where(inner, 2.0 * here, here).astype(jnp.bfloat16)
            lagged = jnp.where(block > 0, before, 0.0) + jnp.where(block < blocks - 1, after, 0.0)
            lagged = lagged.astype(jnp.bfloat16)
            for stream, out_ref in enumerate(out_refs):
                out_ref[places_ref[stream, block], :, :width] = weighted
                out_ref[places_ref[stream, block], :, width:] = lagged

    pl.when(map_ref[0] < blocks)(lambda: fill(own_ref, 0))
    pl.when(map_ref[0] >= blocks)(lambda: fill(passed_ref, blocks))


def lagged_columns(block_map, places, own, passed):
    blocks, frames, width = own.shape
    out = jax.ShapeDtypeStruct((blocks, frames, 2 * width), jnp.bfloat16)
    return pl.pallas_call(
        column_kernel,
        out_shape=(out, out),
        in_specs=[pl.BlockSpec(memory_space=pltpu.SMEM)] * 2 + [pl.BlockSpec(memory_space=pltpu.VMEM)] * 2,
        out_specs=[pl.BlockSpec(memory_space=pltpu.VMEM)] * 2,
        compiler_params=pltpu.CompilerParams(vmem_limit_bytes=20 * MIB),
        cost_estimate=pl.CostEstimate(flops=16 * own.size, bytes_accessed=12 * own.size, transcendentals=0),
    )(block_map, places, own, passed)


def product_kernel(count, factor, started, *refs):
    pieces, columns_ref = refs[:count], refs[count]
    outs = refs[-2:]
    width = outs[0].shape[1]
    left = jnp.concatenate([piece[...].reshape(-1, piece.shape[2]) for piece in pieces], axis=0)
    right = columns_ref[...].reshape(left.shape[0], 2 * width)
    sums = lax.dot_general(left, right, (((0,), (0,)), ((), ())), preferred_element_type=jnp.float32)
    for number, ref in enumerate(outs):
        part = sums[:, number * width : (number + 1) * width]
        ref[...] = (part + refs[count + 1 + number][...]) * factor if started else part


def products(pieces, columns, column_start, start=None, row_start=0, rows=None, factor=1.0, previous=()):
    _, frames, double = columns.shape
    width = double // 2
    features = pieces[0].shape[2]
    first = row_start // TILE
    started = start is not None
    out = jax.ShapeDtypeStruct((rows if started else features, width), jnp.float32)
    count = len(pieces)
    blocks = sum(piece.shape[0] for piece in pieces)
    in_specs = [pl.BlockSpec((piece.shape[0], frames, TILE), lambda i: (0, 0, i)) for piece in pieces]
    in_specs += [
        pl.BlockSpec(
            (blocks, frames, double), lambda i: (column_start // blocks, 0, 0), pipeline_mode=pl.Buffered(1)
        )
    ]
    in_specs += [pl.BlockSpec((TILE, width), lambda i: (i, 0))] * (2 * started)
    in_specs += [pl.BlockSpec(memory_space=pl.ANY)] * len(previous)
    return pl.pallas_call(
        lambda *refs: product_kernel(count, factor, started, *refs),
        grid=(features // TILE,),
        in_specs=in_specs,
        out_specs=[pl.BlockSpec((TILE, width), lambda i: (first + i, 0))] * 2,
        out_shape=(out, out),
        input_output_aliases={count + 3 + n: n for n in range(len(previous))},
        compiler_params=pltpu.CompilerParams(vmem_limit_bytes=16 * MIB),
        cost_estimate=pl.CostEstimate(
            flops=4 * features * blocks * frames * double,
            bytes_accessed=features * double * (8 if started else 4) + blocks * frames * (features + double) * 2,
            transcendentals=0,
        ),
    )(*pieces, columns, *(start or ()), *previous)


def plane_kernel(own_ref, behind_ref, ahead_ref, first_ref, last_ref, out_ref):
    for number, far_ref in enumerate((first_ref, last_ref)):
        for at, block in enumerate((own_ref[number], behind_ref[number], ahead_ref[number], far_ref[...])):
            out_ref[4 * number + at] = block


def plane_of(own, behind, ahead, far):
    return pl.pallas_call(
        plane_kernel,
        out_shape=jax.ShapeDtypeStruct((8, *own.shape[1:]), own.dtype),
        in_specs=[pl.BlockSpec(memory_space=pltpu.VMEM)] * 5,
        out_specs=pl.BlockSpec(memory_space=pltpu.VMEM),
        compiler_params=pltpu.CompilerParams(vmem_limit_bytes=16 * MIB),
        cost_estimate=pl.CostEstimate(flops=0, bytes_accessed=16 * own.size, transcendentals=0),
    )(own, behind, ahead, *far)


def moved(array, axis, by):
    length = lax.axis_size(axis)
    return lax.ppermute(array, axis, [(i, (i + by) % length) for i in range(length)])


def summed(array):
    for axis in ("x", "z", "yl"):
        steps = range(1, lax.axis_size(axis))
        array = sum([moved(array, axis, by) for by in steps], start=array)
    return array


OFFSETS = (0, -1, 1, 2)


def near_blocks(block, axis):
    return moved(block, axis, 1), moved(block, axis, -1)


def far_block(behind, ahead, axis):
    half = behind.shape[0] // 2
    return moved(behind[:half], axis, 1), moved(ahead[half:], axis, -1)


def block_places(first, second, place):
    def number(at, own):
        ahead = (at - own) % 4
        return jnp.where(ahead == 0, 0, jnp.where(ahead == 3, 1, ahead + 1))

    places = []
    for block in range(32):
        at = {"z": (block // 4) % 4, "x": block % 4}
        partner = jnp.where(place["yl"] == block // 16, 0, 4)
        places.append(
            number(at[second], place[second]) * 8 + partner + number(at[first], place[first])
        )
    return jnp.stack(places).astype(jnp.int32)


def columns_along_x(centered, place):
    frames, features = centered.shape
    by_owner = jnp.transpose(centered.reshape(frames, 2, 4, features // 8), (2, 1, 0, 3))
    along_x = [lax.dynamic_index_in_dim(by_owner, place["x"], 0, keepdims=False)]
    for by in (1, 2, 3):
        piece = lax.dynamic_index_in_dim(by_owner, (place["x"] + by) % 4, 0, keepdims=False)
        along_x.append(moved(piece, "x", by))
    return along_x


def columns_along_z(along_x, place):
    along_x = jnp.stack(along_x)
    along_z = [lax.dynamic_index_in_dim(along_x, place["z"] % 2, 1, keepdims=False)]
    for by in (1, 2, 3):
        piece = lax.dynamic_index_in_dim(along_x, (place["z"] + by) % 2, 1, keepdims=False)
        pairs = []
        for z in range(4):
            target = (z + by) % 4
            core = target // 2
            pairs.append((z * 2 + core, target * 2 + core))
        along_z.append(lax.ppermute(piece, ("z", "c"), pairs))
    return along_z


def columns_along_y(along_z, moves):
    pairs = []
    for z in range(4):
        for source, target in moves:
            flat = lambda y: (((y % 2) * 4 + z) * 2 + y // 2) * 2 + z // 2
            pairs.append((flat(source), flat(target)))
    return lax.ppermute(along_z, ("yl", "z", "yh", "c"), pairs)


def columns_of_chip(one, two, place):
    both = jnp.stack([one, two])
    pairs = [(z * 2 + z // 2, z * 2 + 1 - z // 2) for z in range(4)]
    passed = lax.ppermute(both, ("z", "c"), pairs)
    skipped = jnp.where(place["z"] // 2 == place["c"], 0, 32)
    order = []
    for block in range(32):
        y, z, x = block // 16, (block // 4) % 4, block % 4
        group = jnp.where(y == 1 - place["yh"], 0, 1)
        order.append(skipped + group * 16 + ((place["z"] - z) % 4) * 4 + (place["x"] - x) % 4)
    own, passed = [part.reshape(32, *part.shape[3:]) for part in (both, passed)]
    return own, passed, jnp.stack(order).astype(jnp.int32)


def together(*groups):
    return lax.optimization_barrier(groups)


def per_device(coords, set_a, set_b):
    place = {axis: lax.axis_index(axis) for axis in ("yl", "z", "x", "yh", "c")}
    frames, _, atoms, residues = coords.shape
    feat_index = place["yh"] * 2 + place["c"]
    time_index = place["yl"] * 16 + place["z"] * 4 + place["x"]
    rows_a = set_a.shape[0] // 4
    pairs = frames * 32 - LAG
    edge = jnp.logical_or(time_index == 0, time_index == 31)
    index_a = lax.dynamic_slice_in_dim(set_a, feat_index * rows_a, rows_a)
    chosen = jnp.concatenate([set_b, index_a, jnp.zeros((128 - rows_a,), jnp.int32)])
    weight = jnp.broadcast_to(jnp.where(edge, 1, 2).astype(jnp.int32), (256,))
    indices = jnp.stack([chosen, weight, *([weight] * 6)])
    atoms_first = jnp.transpose(coords, (1, 2, 0, 3)).reshape(3 * atoms, frames, residues)

    lifted, sums = contact_features(rows_a, indices, atoms_first)
    centered = (lifted - summed(sums) / (2.0 * pairs)).astype(jnp.bfloat16)

    rows = rows_a * 128
    half = rows // 2
    ways = (("x", "z"), ("z", "x"))
    taken = (slice(0, half), slice(half, rows))

    partner = moved(centered, "yl", 1)
    along_x = columns_along_x(centered, place)
    partner, along_x = together(partner, along_x)

    pairs_of = [jnp.stack([centered[:, part], partner[:, part]]) for part in taken]
    pair_near = [near_blocks(pair, way[0]) for pair, way in zip(pairs_of, ways)]
    along_z = jnp.stack(columns_along_z(along_x, place))
    pair_near, along_z, pairs_of = together(pair_near, along_z, pairs_of)

    far = [
        (moved(behind[0], way[0], 1), moved(ahead[1], way[0], -1)) for (behind, ahead), way in zip(pair_near, ways)
    ]
    two = columns_along_y(along_z, [(1, 2), (2, 1)])
    far, along_z, two = together(far, along_z, two)

    planes = [plane_of(pairs_of[n], *pair_near[n], far[n]) for n in range(2)]
    planes, along_z = together(planes, along_z)
    near = [near_blocks(plane, way[1]) for plane, way in zip(planes, ways)]
    one = columns_along_y(along_z, [(0, 2), (1, 0), (2, 3), (3, 1)])
    two = jnp.where(place["yl"] == place["yh"], along_z, two)
    own_cols, passed_cols, col_order = columns_of_chip(one, two, place)
    places = jnp.stack([block_places(*way, place) for way in ways])
    columns = lagged_columns(col_order, places, own_cols, passed_cols)

    last = [far_block(*blocks, way[1]) for blocks, way in zip(near, ways)]
    starts = [products([planes[n], *near[n]], columns[n], 0) for n in range(2)]
    starts, last = together(starts, last)
    results = ()
    for n in range(2):
        results = products(last[n], columns[n], 24, starts[n], n * half, rows, 0.5 / pairs, results)
    return results


def solution(mesh):
    fine = Mesh(mesh.devices.reshape(2, 4, 4, 2, 2), ("yl", "z", "x", "yh", "c"))
    time_axes, feat_axes = ("yl", "z", "x"), ("yh", "c")
    return jax.shard_map(
        per_device,
        mesh=fine,
        in_specs=(P(time_axes, None, None, None), P(), P()),
        out_specs=(P(feat_axes, time_axes), P(feat_axes, time_axes)),
        check_vma=False,
    )
```

```python
import jax
import jax.numpy as jnp
from jax import lax
from jax.experimental import pallas as pl
from jax.experimental.pallas import tpu as pltpu
from jax.sharding import Mesh, PartitionSpec as P

LAG = 64
contact_radius = 1.2
contact_width = 0.25
TILE = 512
MIB = 1 << 20


def feature_kernel(index_ref, coords_ref, lifted_ref, sums_ref, chosen):
    rows_all, residues = coords_ref.shape
    frames, width = lifted_ref.shape
    pieces = rows_all // frames
    atoms = pieces // 3
    scale = 0.5 / contact_width
    shift = contact_radius * scale

    numbers = lax.broadcasted_iota(jnp.int32, (residues, 256), 0)
    one_hot = jnp.where(numbers == index_ref[0:1, :], scale, 0.0).astype(jnp.bfloat16)

    @pl.loop(0, 3)
    def _(component):
        rows = pl.ds(pl.multiple_of(component * (atoms * frames), atoms * frames), atoms * frames)
        whole = coords_ref[rows, :]
        high = whole.astype(jnp.bfloat16)
        rest = whole - high.astype(jnp.float32)
        middle = rest.astype(jnp.bfloat16)
        low = (rest - middle.astype(jnp.float32)).astype(jnp.bfloat16)
        parts = [jnp.dot(part, one_hot, preferred_element_type=jnp.float32) for part in (high, middle, low)]
        chosen[rows, :] = (parts[0] + parts[1]) + parts[2]

    @pl.loop(0, frames // 8)
    def _(octet):
        start = pl.multiple_of(octet * 8, 8)
        for residue in range(width // 128):
            totals = [None, None]
            for p in range(atoms):
                ax, ay, az = [
                    jnp.broadcast_to(
                        chosen[pl.ds((c * atoms + p) * frames + start, 8), 128 + residue : 129 + residue], (8, 128)
                    )
                    for c in range(3)
                ]
                for q in range(atoms):
                    bx, by, bz = [chosen[pl.ds((c * atoms + q) * frames + start, 8), :128] for c in range(3)]
                    dx, dy, dz = ax - bx, ay - by, az - bz
                    square = jnp.maximum(dx * dx + dy * dy + dz * dz, 1e-30)
                    value = jnp.tanh(shift - square * lax.rsqrt(square))
                    totals[q % 2] = value if totals[q % 2] is None else totals[q % 2] + value
            features = (totals[0] + totals[1] + float(atoms * atoms)) * (0.5 / atoms)
            lifted_ref[pl.ds(start, 8), residue * 128 : (residue + 1) * 128] = features

    weight = index_ref[1:2, 0:1].astype(jnp.float32)
    sums_ref[...] = jnp.sum(lifted_ref[...], axis=0, keepdims=True) * weight


def contact_features(count, indices, coords):
    pieces, frames, residues = coords.shape
    width = count * 128
    pairs = frames * width * (pieces // 3) ** 2
    return pl.pallas_call(
        feature_kernel,
        out_shape=(
            jax.ShapeDtypeStruct((frames, width), jnp.float32),
            jax.ShapeDtypeStruct((1, width), jnp.float32),
        ),
        in_specs=[pl.BlockSpec(memory_space=pltpu.VMEM)] * 2,
        out_specs=[pl.BlockSpec(memory_space=pltpu.VMEM)] * 2,
        scratch_shapes=[pltpu.VMEM((pieces * frames, 256), jnp.float32)],
        compiler_params=pltpu.CompilerParams(vmem_limit_bytes=24 * MIB),
        cost_estimate=pl.CostEstimate(flops=pairs * 12, bytes_accessed=4 * MIB, transcendentals=2 * pairs),
    )(indices, coords.reshape(pieces * frames, residues))


def column_kernel(map_ref, places_ref, own_ref, passed_ref, *out_refs):
    blocks, frames, width = own_ref.shape

    def fill(cols_ref, skipped):
        def block_at(number):
            return cols_ref[map_ref[number] - skipped].astype(jnp.float32)

        @pl.loop(0, blocks)
        def _(block):
            here = block_at(block)
            before = block_at(jnp.maximum(block - 1, 0))
            after = block_at(jnp.minimum(block + 1, blocks - 1))
            inner = jnp.logical_and(block > 0, block < blocks - 1)
            weighted = jnp.where(inner, 2.0 * here, here).astype(jnp.bfloat16)
            lagged = jnp.where(block > 0, before, 0.0) + jnp.where(block < blocks - 1, after, 0.0)
            lagged = lagged.astype(jnp.bfloat16)
            for stream, out_ref in enumerate(out_refs):
                out_ref[places_ref[stream, block], :, :width] = weighted
                out_ref[places_ref[stream, block], :, width:] = lagged

    pl.when(map_ref[0] < blocks)(lambda: fill(own_ref, 0))
    pl.when(map_ref[0] >= blocks)(lambda: fill(passed_ref, blocks))


def lagged_columns(block_map, places, own, passed):
    blocks, frames, width = own.shape
    out = jax.ShapeDtypeStruct((blocks, frames, 2 * width), jnp.bfloat16)
    return pl.pallas_call(
        column_kernel,
        out_shape=(out, out),
        in_specs=[pl.BlockSpec(memory_space=pltpu.SMEM)] * 2 + [pl.BlockSpec(memory_space=pltpu.VMEM)] * 2,
        out_specs=[pl.BlockSpec(memory_space=pltpu.VMEM)] * 2,
        compiler_params=pltpu.CompilerParams(vmem_limit_bytes=20 * MIB),
        cost_estimate=pl.CostEstimate(flops=16 * own.size, bytes_accessed=12 * own.size, transcendentals=0),
    )(block_map, places, own, passed)


def product_kernel(count, factor, started, *refs):
    pieces, columns_ref = refs[:count], refs[count]
    outs = refs[-2:]
    width = outs[0].shape[1]
    left = jnp.concatenate([piece[...].reshape(-1, piece.shape[2]) for piece in pieces], axis=0)
    right = columns_ref[...].reshape(left.shape[0], 2 * width)
    sums = lax.dot_general(left, right, (((0,), (0,)), ((), ())), preferred_element_type=jnp.float32)
    for number, ref in enumerate(outs):
        part = sums[:, number * width : (number + 1) * width]
        ref[...] = (part + refs[count + 1 + number][...]) * factor if started else part


def products(pieces, columns, column_start, start=None, row_start=0, rows=None, factor=1.0, previous=()):
    _, frames, double = columns.shape
    width = double // 2
    features = pieces[0].shape[2]
    first = row_start // TILE
    started = start is not None
    out = jax.ShapeDtypeStruct((rows if started else features, width), jnp.float32)
    count = len(pieces)
    blocks = sum(piece.shape[0] for piece in pieces)
    in_specs = [pl.BlockSpec((piece.shape[0], frames, TILE), lambda i: (0, 0, i)) for piece in pieces]
    in_specs += [
        pl.BlockSpec(
            (blocks, frames, double), lambda i: (column_start // blocks, 0, 0), pipeline_mode=pl.Buffered(1)
        )
    ]
    in_specs += [pl.BlockSpec((TILE, width), lambda i: (i, 0))] * (2 * started)
    in_specs += [pl.BlockSpec(memory_space=pl.ANY)] * len(previous)
    return pl.pallas_call(
        lambda *refs: product_kernel(count, factor, started, *refs),
        grid=(features // TILE,),
        in_specs=in_specs,
        out_specs=[pl.BlockSpec((TILE, width), lambda i: (first + i, 0))] * 2,
        out_shape=(out, out),
        input_output_aliases={count + 3 + n: n for n in range(len(previous))},
        compiler_params=pltpu.CompilerParams(vmem_limit_bytes=16 * MIB),
        cost_estimate=pl.CostEstimate(
            flops=4 * features * blocks * frames * double,
            bytes_accessed=features * double * (8 if started else 4) + blocks * frames * (features + double) * 2,
            transcendentals=0,
        ),
    )(*pieces, columns, *(start or ()), *previous)


def plane_kernel(own_ref, behind_ref, ahead_ref, first_ref, last_ref, out_ref):
    for number, far_ref in enumerate((first_ref, last_ref)):
        for at, block in enumerate((own_ref[number], behind_ref[number], ahead_ref[number], far_ref[...])):
            out_ref[4 * number + at] = block


def plane_of(own, behind, ahead, far):
    return pl.pallas_call(
        plane_kernel,
        out_shape=jax.ShapeDtypeStruct((8, *own.shape[1:]), own.dtype),
        in_specs=[pl.BlockSpec(memory_space=pltpu.VMEM)] * 5,
        out_specs=pl.BlockSpec(memory_space=pltpu.VMEM),
        compiler_params=pltpu.CompilerParams(vmem_limit_bytes=16 * MIB),
        cost_estimate=pl.CostEstimate(flops=0, bytes_accessed=16 * own.size, transcendentals=0),
    )(own, behind, ahead, *far)


def moved(array, axis, by):
    length = lax.axis_size(axis)
    return lax.ppermute(array, axis, [(i, (i + by) % length) for i in range(length)])


def summed(array):
    for axis in ("x", "z", "yl"):
        steps = range(1, lax.axis_size(axis))
        array = sum([moved(array, axis, by) for by in steps], start=array)
    return array


OFFSETS = (0, -1, 1, 2)


def near_blocks(block, axis):
    return moved(block, axis, 1), moved(block, axis, -1)


def far_block(behind, ahead, axis):
    half = behind.shape[0] // 2
    return moved(behind[:half], axis, 1), moved(ahead[half:], axis, -1)


def block_places(first, second, place):
    def number(at, own):
        ahead = (at - own) % 4
        return jnp.where(ahead == 0, 0, jnp.where(ahead == 3, 1, ahead + 1))

    places = []
    for block in range(32):
        at = {"z": (block // 4) % 4, "x": block % 4}
        partner = jnp.where(place["yl"] == block // 16, 0, 4)
        places.append(
            number(at[second], place[second]) * 8 + partner + number(at[first], place[first])
        )
    return jnp.stack(places).astype(jnp.int32)


def columns_along_x(centered, place):
    frames, features = centered.shape
    by_owner = jnp.transpose(centered.reshape(frames, 2, 4, features // 8), (2, 1, 0, 3))
    along_x = [lax.dynamic_index_in_dim(by_owner, place["x"], 0, keepdims=False)]
    for by in (1, 2, 3):
        piece = lax.dynamic_index_in_dim(by_owner, (place["x"] + by) % 4, 0, keepdims=False)
        along_x.append(moved(piece, "x", by))
    return along_x


def columns_along_z(along_x, place):
    along_x = jnp.stack(along_x)
    along_z = [lax.dynamic_index_in_dim(along_x, place["z"] % 2, 1, keepdims=False)]
    for by in (1, 2, 3):
        piece = lax.dynamic_index_in_dim(along_x, (place["z"] + by) % 2, 1, keepdims=False)
        pairs = []
        for z in range(4):
            target = (z + by) % 4
            core = target // 2
            pairs.append((z * 2 + core, target * 2 + core))
        along_z.append(lax.ppermute(piece, ("z", "c"), pairs))
    return along_z


def columns_along_y(along_z, moves):
    pairs = []
    for z in range(4):
        for source, target in moves:
            flat = lambda y: (((y % 2) * 4 + z) * 2 + y // 2) * 2 + z // 2
            pairs.append((flat(source), flat(target)))
    return lax.ppermute(along_z, ("yl", "z", "yh", "c"), pairs)


def columns_of_chip(one, two, place):
    both = jnp.stack([one, two])
    pairs = [(z * 2 + z // 2, z * 2 + 1 - z // 2) for z in range(4)]
    passed = lax.ppermute(both, ("z", "c"), pairs)
    skipped = jnp.where(place["z"] // 2 == place["c"], 0, 32)
    order = []
    for block in range(32):
        y, z, x = block // 16, (block // 4) % 4, block % 4
        group = jnp.where(y == 1 - place["yh"], 0, 1)
        order.append(skipped + group * 16 + ((place["z"] - z) % 4) * 4 + (place["x"] - x) % 4)
    own, passed = [part.reshape(32, *part.shape[3:]) for part in (both, passed)]
    return own, passed, jnp.stack(order).astype(jnp.int32)


def together(*groups):
    return lax.optimization_barrier(groups)


def per_device(coords, set_a, set_b):
    place = {axis: lax.axis_index(axis) for axis in ("yl", "z", "x", "yh", "c")}
    frames, _, atoms, residues = coords.shape
    feat_index = place["yh"] * 2 + place["c"]
    time_index = place["yl"] * 16 + place["z"] * 4 + place["x"]
    rows_a = set_a.shape[0] // 4
    pairs = frames * 32 - LAG
    edge = jnp.logical_or(time_index == 0, time_index == 31)
    index_a = lax.dynamic_slice_in_dim(set_a, feat_index * rows_a, rows_a)
    chosen = jnp.concatenate([set_b, index_a, jnp.zeros((128 - rows_a,), jnp.int32)])
    weight = jnp.broadcast_to(jnp.where(edge, 1, 2).astype(jnp.int32), (256,))
    indices = jnp.stack([chosen, weight, *([weight] * 6)])
    atoms_first = jnp.transpose(coords, (1, 2, 0, 3)).reshape(3 * atoms, frames, residues)

    lifted, sums = contact_features(rows_a, indices, atoms_first)
    centered = (lifted - summed(sums) / (2.0 * pairs)).astype(jnp.bfloat16)

    rows = rows_a * 128
    half = rows // 2
    ways = (("x", "z"), ("z", "x"))
    taken = (slice(0, half), slice(half, rows))

    partner = moved(centered, "yl", 1)
    along_x = columns_along_x(centered, place)

    pairs_of = [jnp.stack([centered[:, part], partner[:, part]]) for part in taken]
    pair_near = [near_blocks(pair, way[0]) for pair, way in zip(pairs_of, ways)]
    along_z = jnp.stack(columns_along_z(along_x, place))
    pair_near, along_z = together(pair_near, along_z)

    far = [
        (moved(behind[0], way[0], 1), moved(ahead[1], way[0], -1)) for (behind, ahead), way in zip(pair_near, ways)
    ]
    two = columns_along_y(along_z, [(1, 2), (2, 1)])
    far, along_z, two = together(far, along_z, two)

    planes = [plane_of(pairs_of[n], *pair_near[n], far[n]) for n in range(2)]
    planes, along_z = together(planes, along_z)
    near = [near_blocks(plane, way[1]) for plane, way in zip(planes, ways)]
    one = columns_along_y(along_z, [(0, 2), (1, 0), (2, 3), (3, 1)])
    two = jnp.where(place["yl"] == place["yh"], along_z, two)
    own_cols, passed_cols, col_order = columns_of_chip(one, two, place)
    places = jnp.stack([block_places(*way, place) for way in ways])
    columns = lagged_columns(col_order, places, own_cols, passed_cols)

    last = [far_block(*blocks, way[1]) for blocks, way in zip(near, ways)]
    starts = [products([planes[n], *near[n]], columns[n], 0) for n in range(2)]
    starts, last = together(starts, last)
    results = ()
    for n in range(2):
        results = products(last[n], columns[n], 24, starts[n], n * half, rows, 0.5 / pairs, results)
    return results


def solution(mesh):
    fine = Mesh(mesh.devices.reshape(2, 4, 4, 2, 2), ("yl", "z", "x", "yh", "c"))
    time_axes, feat_axes = ("yl", "z", "x"), ("yh", "c")
    return jax.shard_map(
        per_device,
        mesh=fine,
        in_specs=(P(time_axes, None, None, None), P(), P()),
        out_specs=(P(feat_axes, time_axes), P(feat_axes, time_axes)),
        check_vma=False,
    )
```

```python
import jax
import jax.numpy as jnp
from jax import lax
from jax.experimental import pallas as pl
from jax.experimental.pallas import tpu as pltpu
from jax.sharding import Mesh, PartitionSpec as P

LAG = 64
contact_radius = 1.2
contact_width = 0.25
TILE = 512
MIB = 1 << 20


def feature_kernel(index_ref, coords_ref, lifted_ref, sums_ref, chosen):
    rows_all, residues = coords_ref.shape
    frames, width = lifted_ref.shape
    pieces = rows_all // frames
    atoms = pieces // 3
    scale = 0.5 / contact_width
    shift = contact_radius * scale

    numbers = lax.broadcasted_iota(jnp.int32, (residues, 256), 0)
    one_hot = jnp.where(numbers == index_ref[0:1, :], scale, 0.0).astype(jnp.bfloat16)

    @pl.loop(0, 3)
    def _(component):
        rows = pl.ds(pl.multiple_of(component * (atoms * frames), atoms * frames), atoms * frames)
        whole = coords_ref[rows, :]
        high = whole.astype(jnp.bfloat16)
        rest = whole - high.astype(jnp.float32)
        middle = rest.astype(jnp.bfloat16)
        low = (rest - middle.astype(jnp.float32)).astype(jnp.bfloat16)
        parts = [jnp.dot(part, one_hot, preferred_element_type=jnp.float32) for part in (high, middle, low)]
        chosen[rows, :] = (parts[0] + parts[1]) + parts[2]

    @pl.loop(0, frames // 8)
    def _(octet):
        start = pl.multiple_of(octet * 8, 8)
        for residue in range(width // 128):
            totals = [None, None]
            for p in range(atoms):
                ax, ay, az = [
                    jnp.broadcast_to(
                        chosen[pl.ds((c * atoms + p) * frames + start, 8), 128 + residue : 129 + residue], (8, 128)
                    )
                    for c in range(3)
                ]
                for q in range(atoms):
                    bx, by, bz = [chosen[pl.ds((c * atoms + q) * frames + start, 8), :128] for c in range(3)]
                    dx, dy, dz = ax - bx, ay - by, az - bz
                    square = jnp.maximum(dx * dx + dy * dy + dz * dz, 1e-30)
                    value = jnp.tanh(shift - square * lax.rsqrt(square))
                    totals[q % 2] = value if totals[q % 2] is None else totals[q % 2] + value
            features = (totals[0] + totals[1] + float(atoms * atoms)) * (0.5 / atoms)
            lifted_ref[pl.ds(start, 8), residue * 128 : (residue + 1) * 128] = features

    weight = index_ref[1:2, 0:1].astype(jnp.float32)
    sums_ref[...] = jnp.sum(lifted_ref[...], axis=0, keepdims=True) * weight


def contact_features(count, indices, coords):
    pieces, frames, residues = coords.shape
    width = count * 128
    pairs = frames * width * (pieces // 3) ** 2
    return pl.pallas_call(
        feature_kernel,
        out_shape=(
            jax.ShapeDtypeStruct((frames, width), jnp.float32),
            jax.ShapeDtypeStruct((1, width), jnp.float32),
        ),
        in_specs=[pl.BlockSpec(memory_space=pltpu.VMEM)] * 2,
        out_specs=[pl.BlockSpec(memory_space=pltpu.VMEM)] * 2,
        scratch_shapes=[pltpu.VMEM((pieces * frames, 256), jnp.float32)],
        compiler_params=pltpu.CompilerParams(vmem_limit_bytes=24 * MIB),
        cost_estimate=pl.CostEstimate(flops=pairs * 12, bytes_accessed=4 * MIB, transcendentals=2 * pairs),
    )(indices, coords.reshape(pieces * frames, residues))


def column_kernel(map_ref, places_ref, own_ref, passed_ref, *out_refs):
    blocks, frames, width = own_ref.shape

    def fill(cols_ref, skipped):
        def block_at(number):
            return cols_ref[map_ref[number] - skipped].astype(jnp.float32)

        @pl.loop(0, blocks, unroll=4)
        def _(block):
            here = block_at(block)
            before = block_at(jnp.maximum(block - 1, 0))
            after = block_at(jnp.minimum(block + 1, blocks - 1))
            inner = jnp.logical_and(block > 0, block < blocks - 1)
            weighted = (here * jnp.where(inner, 2.0, 1.0)).astype(jnp.bfloat16)
            lagged = jnp.where(block > 0, before, 0.0) + jnp.where(block < blocks - 1, after, 0.0)
            lagged = lagged.astype(jnp.bfloat16)
            for stream, out_ref in enumerate(out_refs):
                out_ref[places_ref[stream, block], :, :width] = weighted
                out_ref[places_ref[stream, block], :, width:] = lagged

    pl.when(map_ref[0] < blocks)(lambda: fill(own_ref, 0))
    pl.when(map_ref[0] >= blocks)(lambda: fill(passed_ref, blocks))


def lagged_columns(block_map, places, own, passed):
    blocks, frames, width = own.shape
    out = jax.ShapeDtypeStruct((blocks, frames, 2 * width), jnp.bfloat16)
    return pl.pallas_call(
        column_kernel,
        out_shape=(out, out),
        in_specs=[pl.BlockSpec(memory_space=pltpu.SMEM)] * 2 + [pl.BlockSpec(memory_space=pltpu.VMEM)] * 2,
        out_specs=[pl.BlockSpec(memory_space=pltpu.VMEM)] * 2,
        compiler_params=pltpu.CompilerParams(vmem_limit_bytes=20 * MIB),
        cost_estimate=pl.CostEstimate(flops=16 * own.size, bytes_accessed=12 * own.size, transcendentals=0),
    )(block_map, places, own, passed)


def product_kernel(count, factor, started, *refs):
    pieces, columns_ref = refs[:count], refs[count]
    outs = refs[-2:]
    width = outs[0].shape[1]
    left = jnp.concatenate([piece[...].reshape(-1, piece.shape[2]) for piece in pieces], axis=0)
    right = columns_ref[...].reshape(left.shape[0], 2 * width)
    sums = lax.dot_general(left, right, (((0,), (0,)), ((), ())), preferred_element_type=jnp.float32)
    for number, ref in enumerate(outs):
        part = sums[:, number * width : (number + 1) * width]
        ref[...] = (part + refs[count + 1 + number][...]) * factor if started else part


def products(pieces, columns, column_start, start=None, row_start=0, rows=None, factor=1.0, previous=()):
    _, frames, double = columns.shape
    width = double // 2
    features = pieces[0].shape[2]
    first = row_start // TILE
    started = start is not None
    out = jax.ShapeDtypeStruct((rows if started else features, width), jnp.float32)
    count = len(pieces)
    blocks = sum(piece.shape[0] for piece in pieces)
    in_specs = [pl.BlockSpec((piece.shape[0], frames, TILE), lambda i: (0, 0, i)) for piece in pieces]
    in_specs += [
        pl.BlockSpec(
            (blocks, frames, double), lambda i: (column_start // blocks, 0, 0), pipeline_mode=pl.Buffered(1)
        )
    ]
    in_specs += [pl.BlockSpec((TILE, width), lambda i: (i, 0))] * (2 * started)
    in_specs += [pl.BlockSpec(memory_space=pl.ANY)] * len(previous)
    return pl.pallas_call(
        lambda *refs: product_kernel(count, factor, started, *refs),
        grid=(features // TILE,),
        in_specs=in_specs,
        out_specs=[pl.BlockSpec((TILE, width), lambda i: (first + i, 0))] * 2,
        out_shape=(out, out),
        input_output_aliases={count + 3 + n: n for n in range(len(previous))},
        compiler_params=pltpu.CompilerParams(vmem_limit_bytes=16 * MIB),
        cost_estimate=pl.CostEstimate(
            flops=4 * features * blocks * frames * double,
            bytes_accessed=features * double * (8 if started else 4) + blocks * frames * (features + double) * 2,
            transcendentals=0,
        ),
    )(*pieces, columns, *(start or ()), *previous)


def plane_kernel(own_ref, behind_ref, ahead_ref, first_ref, last_ref, out_ref):
    for number, far_ref in enumerate((first_ref, last_ref)):
        for at, block in enumerate((own_ref[number], behind_ref[number], ahead_ref[number], far_ref[...])):
            out_ref[4 * number + at] = block


def plane_of(own, behind, ahead, far):
    return pl.pallas_call(
        plane_kernel,
        out_shape=jax.ShapeDtypeStruct((8, *own.shape[1:]), own.dtype),
        in_specs=[pl.BlockSpec(memory_space=pltpu.VMEM)] * 5,
        out_specs=pl.BlockSpec(memory_space=pltpu.VMEM),
        compiler_params=pltpu.CompilerParams(vmem_limit_bytes=16 * MIB),
        cost_estimate=pl.CostEstimate(flops=0, bytes_accessed=16 * own.size, transcendentals=0),
    )(own, behind, ahead, *far)


def moved(array, axis, by):
    length = lax.axis_size(axis)
    return lax.ppermute(array, axis, [(i, (i + by) % length) for i in range(length)])


def summed(array):
    for axis in ("x", "z", "yl"):
        steps = range(1, lax.axis_size(axis))
        array = sum([moved(array, axis, by) for by in steps], start=array)
    return array


OFFSETS = (0, -1, 1, 2)


def near_blocks(block, axis):
    return moved(block, axis, 1), moved(block, axis, -1)


def far_block(behind, ahead, axis):
    half = behind.shape[0] // 2
    return moved(behind[:half], axis, 1), moved(ahead[half:], axis, -1)


def block_places(first, second, place):
    def number(at, own):
        ahead = (at - own) % 4
        return jnp.where(ahead == 0, 0, jnp.where(ahead == 3, 1, ahead + 1))

    places = []
    for block in range(32):
        at = {"z": (block // 4) % 4, "x": block % 4}
        partner = jnp.where(place["yl"] == block // 16, 0, 4)
        places.append(
            number(at[second], place[second]) * 8 + partner + number(at[first], place[first])
        )
    return jnp.stack(places).astype(jnp.int32)


def columns_along_x(centered, place):
    frames, features = centered.shape
    by_owner = jnp.transpose(centered.reshape(frames, 2, 4, features // 8), (2, 1, 0, 3))
    along_x = [lax.dynamic_index_in_dim(by_owner, place["x"], 0, keepdims=False)]
    for by in (1, 2, 3):
        piece = lax.dynamic_index_in_dim(by_owner, (place["x"] + by) % 4, 0, keepdims=False)
        along_x.append(moved(piece, "x", by))
    return along_x


def columns_along_z(along_x, place):
    along_x = jnp.stack(along_x)
    along_z = [lax.dynamic_index_in_dim(along_x, place["z"] % 2, 1, keepdims=False)]
    for by in (1, 2, 3):
        piece = lax.dynamic_index_in_dim(along_x, (place["z"] + by) % 2, 1, keepdims=False)
        pairs = []
        for z in range(4):
            target = (z + by) % 4
            core = target // 2
            pairs.append((z * 2 + core, target * 2 + core))
        along_z.append(lax.ppermute(piece, ("z", "c"), pairs))
    return along_z


def columns_along_y(along_z, moves):
    pairs = []
    for z in range(4):
        for source, target in moves:
            flat = lambda y: (((y % 2) * 4 + z) * 2 + y // 2) * 2 + z // 2
            pairs.append((flat(source), flat(target)))
    return lax.ppermute(along_z, ("yl", "z", "yh", "c"), pairs)


def columns_of_chip(one, two, place):
    both = jnp.stack([one, two])
    pairs = [(z * 2 + z // 2, z * 2 + 1 - z // 2) for z in range(4)]
    passed = lax.ppermute(both, ("z", "c"), pairs)
    skipped = jnp.where(place["z"] // 2 == place["c"], 0, 32)
    order = []
    for block in range(32):
        y, z, x = block // 16, (block // 4) % 4, block % 4
        group = jnp.where(y == 1 - place["yh"], 0, 1)
        order.append(skipped + group * 16 + ((place["z"] - z) % 4) * 4 + (place["x"] - x) % 4)
    own, passed = [part.reshape(32, *part.shape[3:]) for part in (both, passed)]
    return own, passed, jnp.stack(order).astype(jnp.int32)


def together(*groups):
    return lax.optimization_barrier(groups)


def per_device(coords, set_a, set_b):
    place = {axis: lax.axis_index(axis) for axis in ("yl", "z", "x", "yh", "c")}
    frames, _, atoms, residues = coords.shape
    feat_index = place["yh"] * 2 + place["c"]
    time_index = place["yl"] * 16 + place["z"] * 4 + place["x"]
    rows_a = set_a.shape[0] // 4
    pairs = frames * 32 - LAG
    edge = jnp.logical_or(time_index == 0, time_index == 31)
    index_a = lax.dynamic_slice_in_dim(set_a, feat_index * rows_a, rows_a)
    chosen = jnp.concatenate([set_b, index_a, jnp.zeros((128 - rows_a,), jnp.int32)])
    weight = jnp.broadcast_to(jnp.where(edge, 1, 2).astype(jnp.int32), (256,))
    indices = jnp.stack([chosen, weight, *([weight] * 6)])
    atoms_first = jnp.transpose(coords, (1, 2, 0, 3)).reshape(3 * atoms, frames, residues)

    lifted, sums = contact_features(rows_a, indices, atoms_first)
    centered = (lifted - summed(sums) / (2.0 * pairs)).astype(jnp.bfloat16)

    rows = rows_a * 128
    half = rows // 2
    ways = (("x", "z"), ("z", "x"))
    taken = (slice(0, half), slice(half, rows))

    partner = moved(centered, "yl", 1)
    along_x = columns_along_x(centered, place)

    pairs_of = [jnp.stack([centered[:, part], partner[:, part]]) for part in taken]
    pair_near = [near_blocks(pair, way[0]) for pair, way in zip(pairs_of, ways)]
    along_z = jnp.stack(columns_along_z(along_x, place))
    pair_near, along_z = together(pair_near, along_z)

    far = [
        (moved(behind[0], way[0], 1), moved(ahead[1], way[0], -1)) for (behind, ahead), way in zip(pair_near, ways)
    ]
    two = columns_along_y(along_z, [(1, 2), (2, 1)])
    far, along_z, two = together(far, along_z, two)

    planes = [plane_of(pairs_of[n], *pair_near[n], far[n]) for n in range(2)]
    planes, along_z = together(planes, along_z)
    near = [near_blocks(plane, way[1]) for plane, way in zip(planes, ways)]
    one = columns_along_y(along_z, [(0, 2), (1, 0), (2, 3), (3, 1)])
    two = jnp.where(place["yl"] == place["yh"], along_z, two)
    own_cols, passed_cols, col_order = columns_of_chip(one, two, place)
    places = jnp.stack([block_places(*way, place) for way in ways])
    columns = lagged_columns(col_order, places, own_cols, passed_cols)

    last = [far_block(*blocks, way[1]) for blocks, way in zip(near, ways)]
    starts = [products([planes[n], *near[n]], columns[n], 0) for n in range(2)]
    starts, last = together(starts, last)
    results = ()
    for n in range(2):
        results = products(last[n], columns[n], 24, starts[n], n * half, rows, 0.5 / pairs, results)
    return results


def solution(mesh):
    fine = Mesh(mesh.devices.reshape(2, 4, 4, 2, 2), ("yl", "z", "x", "yh", "c"))
    time_axes, feat_axes = ("yl", "z", "x"), ("yh", "c")
    return jax.shard_map(
        per_device,
        mesh=fine,
        in_specs=(P(time_axes, None, None, None), P(), P()),
        out_specs=(P(feat_axes, time_axes), P(feat_axes, time_axes)),
        check_vma=False,
    )
```
